32 devices in a mesh: frame: 2 (over x), rows: 16 (over z, y, core).
Axes of the slice: x: 2, y: 2, z: 4, core: 2. Of those that a mesh axis runs over, the one named last changes fastest.
Arguments:
- interferograms: bfloat16 [600, 256, 256], P(None, ('frame', 'rows')), parts along dimension 1, may hold values from -6 to 6
- pseudo_inverse: bfloat16 [200, 600], replicated, may hold values from -0.25 to 0.25
- date_pairs: int32 [2, 600], replicated, may hold values from 0 to 199, as said below
- ref_pixel: int32 [2], P('frame'), parts along dimension 0, may hold values from 0 to 32767
- band_width: int32 [1], replicated, may hold values from 5 to 60
- prior_mean: float32 [32, 4, 2048], P(('frame', 'rows')), parts along dimension 0, may hold values from -6 to 6
- prior_precision: float32 [32, 4, 2048], P(('frame', 'rows')), parts along dimension 0, may hold values from 20 to 200
Outputs:
- series: bfloat16 [32, 200, 2048], P(('frame', 'rows')), parts along dimension 0
- kalman_state: float32 [32, 4, 2048], P(('frame', 'rows')), parts along dimension 0
- misfit: bfloat16 [32, 2048], P(('frame', 'rows')), parts along dimension 0
The draws below stay inside these ranges and needn't reach their ends.
There are 2 independent parts, one for each index of `frame`. The reference program is written for one: setup_inputs(seed, part) draws one part's arguments, and reference() takes and returns one part's arrays. A program takes and returns all parts, laid end to end along the dimension named above; an argument that names none is the same for every part. Nothing has to cross between parts.
Inputs may be any that keep to these rules, and one draw needn't show every extreme that they name: `date_pairs`: row 0 holds each interferogram's earlier date, row 1 its later date, 1 to 6 dates after the earlier one; some interferogram starts on the first date and some ends on the last.
All inputs are finite; a program needn't handle non-finite values.
Results may differ from the reference program's by a relative error of at most 0.0017.
The reference program's roundings to bfloat16 on the way count: a program that leaves them out, or rounds other values in their place, can miss the bound.
Values may be sent and summed in bfloat16 or wider, within the bound.
A program may use at most 64 MiB of HBM per device.

```python
import math
import jax
import jax.numpy as jnp
from jax import lax

IFGS = 600
DATES = 200
RADIUS = 4
COLS = 256
ROWS_ALL = 128
SLABS = 16
PIX_DEV = 2048
N_ROWS = 16


def draw_date_pairs(key, part):
    first_key, second_key, third_key = jax.random.split(jax.random.fold_in(key, 17), 3)
    earlier = jax.random.randint(first_key, (IFGS,), 0, DATES - 1)
    last_span = jax.random.randint(third_key, (), 1, 7)
    earlier = earlier.at[0].set(0)
    earlier = earlier.at[IFGS - 1].set(DATES - 1 - last_span)
    spans = jnp.minimum(6, DATES - 1 - earlier)
    later_date = earlier + jax.random.randint(second_key, (IFGS,), 1, spans + 1)
    later_date = later_date.at[IFGS - 1].set(DATES - 1)
    return jnp.stack([earlier, later_date]).astype(jnp.int32)


def block_levels(own_key, extent, cuts, smallest, high):
    loudness = 1.0
    for dim, shards_of in cuts:
        draws = jax.random.uniform(jax.random.fold_in(jax.random.fold_in(own_key, 6), dim), (shards_of,), jnp.float32, smallest / len(cuts), high / len(cuts))
        loudness = loudness * jnp.repeat(jnp.exp(draws), extent[dim] // shards_of).reshape((-1,) + (1,) * (len(extent) - 1 - dim))
    return loudness


def bell_draw(stream_key, extent, width, reach, cuts=(), kind=jnp.bfloat16):
    level = block_levels(stream_key, extent, cuts, -0.22, 0.18) if cuts else 1.0
    array = jax.random.normal(stream_key, extent, jnp.float32) * width * level
    return jnp.minimum(jnp.maximum(array, -reach), reach).astype(kind)


def setup_inputs(seed: int = 0, part: int = 0) -> dict:
    streams_of = jax.random.split(jax.random.key(seed), 8)
    part_keys = jax.random.split(jax.random.fold_in(streams_of[7], part), 8)
    return {
        "interferograms": bell_draw(part_keys[0], (IFGS, ROWS_ALL, COLS), 1.0, 6.0, ((1, 16),)),
        "pseudo_inverse": bell_draw(streams_of[1], (DATES, IFGS), IFGS ** -0.5, 0.25),
        "date_pairs": draw_date_pairs(jax.random.fold_in(streams_of[7], 71), part),
        "ref_pixel": jax.random.randint(part_keys[3], (1,), 0, ROWS_ALL * COLS).astype(jnp.int32),
        "band_width": jax.random.randint(streams_of[4], (1,), 5, 61).astype(jnp.int32),
        "prior_mean": bell_draw(part_keys[5], (SLABS, 4, PIX_DEV), 1.0, 6.0, ((0, 16),), jnp.float32),
        "prior_precision": jnp.clip(jnp.exp(math.log(200.0) - 2.3025851 * jax.random.uniform(part_keys[6], (SLABS, 4, PIX_DEV), jnp.float32) ** block_levels(part_keys[6], (SLABS, 4, PIX_DEV), ((0, 16),), -0.2, 0.2)), 20.0, 200.0),
    }


def filter_taps(band_width):
    spread = band_width[0].astype(jnp.float32) / 10.0
    offsets = jnp.arange(-RADIUS, RADIUS + 1).astype(jnp.float32)
    raw_taps = jnp.exp(-offsets * offsets / (2.0 * spread * spread))
    return raw_taps / jnp.sum(raw_taps)

def column_pass(images, kernel_taps):
    values = images.astype(jnp.float32)
    columns = values.shape[2]
    padded = jnp.pad(values, ((0, 0), (0, 0), (RADIUS, RADIUS)))
    summed = kernel_taps[0] * padded[:, :, 0:columns]
    for offset in range(1, 2 * RADIUS + 1):
        summed = summed + kernel_taps[offset] * padded[:, :, offset:offset + columns]
    return summed.astype(jnp.bfloat16)

def row_pass(extended, kernel_taps, height):
    summed = kernel_taps[0] * extended[:, 0:height]
    for offset in range(1, 2 * RADIUS + 1):
        summed = summed + kernel_taps[offset] * extended[:, offset:offset + height]
    return summed

def high_pass(images, kernel_taps):
    smoothed = column_pass(images, kernel_taps)
    smoothed = lax.optimization_barrier(smoothed)
    extended = jnp.pad(smoothed.astype(jnp.float32), ((0, 0), (RADIUS, RADIUS), (0, 0)))
    lowpass = row_pass(extended, kernel_taps, images.shape[1])
    return (images.astype(jnp.float32) - lowpass).astype(jnp.bfloat16)

def design_of(date_pairs):
    date_index = jnp.arange(DATES, dtype=jnp.int32)
    later_date = (date_index[None, :] == date_pairs[1][:, None]).astype(jnp.float32)
    earlier = (date_index[None, :] == date_pairs[0][:, None]).astype(jnp.float32)
    return (later_date - earlier).astype(jnp.bfloat16)

def trend_basis():
    epochs = jnp.arange(DATES).astype(jnp.float32)
    centred = (epochs - (DATES - 1) / 2.0) / DATES
    annual_phase = 2.0 * math.pi * 12.0 / 365.25 * epochs
    constant = jnp.ones_like(epochs)
    return jnp.stack([constant, centred, jnp.cos(annual_phase), jnp.sin(annual_phase)], axis=1)

def reference(interferograms, pseudo_inverse, date_pairs, ref_pixel, band_width, prior_mean, prior_precision):
    kernel_taps = filter_taps(band_width)
    filtered = lax.map(lambda single: high_pass(single[None], kernel_taps)[0], interferograms)
    slab_count = N_ROWS
    slab_cols = COLS // slab_count
    grouped = filtered.reshape(IFGS, ROWS_ALL, slab_count, slab_cols).transpose(2, 0, 1, 3)
    grouped = grouped.reshape(slab_count, IFGS, ROWS_ALL * slab_cols)
    design = design_of(date_pairs)

    def invert_slab(slab_values):
        displacement = jnp.dot(pseudo_inverse.astype(jnp.float32), slab_values.astype(jnp.float32), preferred_element_type=jnp.float32).astype(jnp.bfloat16)
        modelled = jnp.dot(design.astype(jnp.float32), displacement.astype(jnp.float32), preferred_element_type=jnp.float32)
        residual = slab_values.astype(jnp.float32) - modelled
        return (displacement, jnp.mean(residual * residual, axis=0).astype(jnp.bfloat16))
    displacement, misfit = lax.map(invert_slab, grouped)
    ref_index = ref_pixel[0]
    ref_row = ref_index // COLS
    ref_col = ref_index % COLS
    owner_slab = ref_col // slab_cols
    local_pixel = ref_row * slab_cols + ref_col - owner_slab * slab_cols
    ref_series = displacement[owner_slab, :, local_pixel]
    series = (displacement.astype(jnp.float32) - ref_series.astype(jnp.float32)[None, :, None]).astype(jnp.bfloat16)
    trend_rows = trend_basis()
    trend_gram = jnp.dot(trend_rows.T, trend_rows, precision=lax.Precision.HIGHEST)
    identity = jnp.eye(4, dtype=jnp.float32)

    def kalman_slab(members):
        slab_series, slab_misfit, slab_mean, slab_precision = members
        projected = jnp.dot(trend_rows.T, slab_series.astype(jnp.float32), precision=lax.Precision.HIGHEST)
        noise = 0.1 + slab_misfit.astype(jnp.float32)
        matrix = slab_precision.T[:, :, None] * identity[None] + trend_gram[None] / noise[:, None, None]
        right_side = (slab_precision * slab_mean + projected / noise[None]).T[:, :, None]
        return jnp.linalg.solve(matrix, right_side)[:, :, 0].T
    kalman_state = lax.map(kalman_slab, (series, misfit, prior_mean, prior_precision))
    return (series, kalman_state, misfit)
```

```python
import math

import jax
import jax.numpy as jnp
from jax import lax
from jax.sharding import PartitionSpec as P

DATES = 200
RADIUS = 4


def padded_2(cells, sides, width):
    for axis, dim in sides:
        count = lax.axis_size(axis)
        ends = count - 1
        head = lax.slice_in_dim(cells, 0, width, axis=dim)
        tail = lax.slice_in_dim(cells, cells.shape[dim] - width, cells.shape[dim], axis=dim)
        cells = jnp.concatenate(
            [
                lax.ppermute(tail, axis, [(i, (i + 1) % count) for i in range(ends)]),
                cells,
                lax.ppermute(head, axis, [((i + 1) % count, i) for i in range(ends)]),
            ],
            axis=dim,
        )
    return cells


def filter_taps(band_width):
    spread = band_width[0].astype(jnp.float32) / 10.0
    offsets = jnp.arange(-RADIUS, RADIUS + 1).astype(jnp.float32)
    raw_taps = jnp.exp(-offsets * offsets / (2.0 * spread * spread))
    return raw_taps / jnp.sum(raw_taps)


def column_pass(images, kernel_taps):
    values = images.astype(jnp.float32)
    columns = values.shape[2]
    padded = jnp.pad(values, ((0, 0), (0, 0), (RADIUS, RADIUS)))
    summed = kernel_taps[0] * padded[:, :, 0:columns]
    for offset in range(1, 2 * RADIUS + 1):
        summed = summed + kernel_taps[offset] * padded[:, :, offset : offset + columns]
    return summed.astype(jnp.bfloat16)


def row_pass(extended, kernel_taps, height):
    summed = kernel_taps[0] * extended[:, 0:height]
    for offset in range(1, 2 * RADIUS + 1):
        summed = summed + kernel_taps[offset] * extended[:, offset : offset + height]
    return summed


def design_of(date_pairs):
    date_index = jnp.arange(DATES, dtype=jnp.int32)
    later_date = (date_index[None, :] == date_pairs[1][:, None]).astype(jnp.float32)
    earlier = (date_index[None, :] == date_pairs[0][:, None]).astype(jnp.float32)
    return (later_date - earlier).astype(jnp.bfloat16)


def trend_basis():
    epochs = jnp.arange(DATES).astype(jnp.float32)
    centred = (epochs - (DATES - 1) / 2.0) / DATES
    annual_phase = 2.0 * math.pi * 12.0 / 365.25 * epochs
    constant = jnp.ones_like(epochs)
    return jnp.stack([constant, centred, jnp.cos(annual_phase), jnp.sin(annual_phase)], axis=1)


def misfit_of(slab_values, displacement, design):
    modelled = jnp.dot(design, displacement, preferred_element_type=jnp.float32)
    residual = slab_values.astype(jnp.float32) - modelled
    return jnp.mean(residual * residual, axis=0).astype(jnp.bfloat16)


def slab_major(values, slab_count, slab_cols):
    leading, local_rows, columns = values.shape
    split_up = values.reshape(leading, local_rows, slab_count, slab_cols).transpose(2, 0, 1, 3)
    return split_up.reshape(slab_count, leading, local_rows * slab_cols)


def from_sources(arrived):
    sources, leading, piece_len = arrived.shape
    return arrived.transpose(1, 0, 2).reshape(leading, sources * piece_len)


def solve_small(matrix, right_side):
    dimension = len(right_side)
    factor = [[None] * dimension for row_at in range(dimension)]
    for column_at in range(dimension):
        pivot_sq = matrix[column_at][column_at]
        for term_at in range(column_at):
            pivot_sq = pivot_sq - factor[column_at][term_at] * factor[column_at][term_at]
        factor[column_at][column_at] = jnp.sqrt(pivot_sq)
        for row_at in range(column_at + 1, dimension):
            element = matrix[row_at][column_at]
            for term_at in range(column_at):
                element = element - factor[row_at][term_at] * factor[column_at][term_at]
            factor[row_at][column_at] = element / factor[column_at][column_at]
    forward = []
    for row_at in range(dimension):
        element = right_side[row_at]
        for term_at in range(row_at):
            element = element - factor[row_at][term_at] * forward[term_at]
        forward.append(element / factor[row_at][row_at])
    solution = [None] * dimension
    for row_at in reversed(range(dimension)):
        element = forward[row_at]
        for term_at in range(row_at + 1, dimension):
            element = element - factor[term_at][row_at] * solution[term_at]
        solution[row_at] = element / factor[row_at][row_at]
    return solution


def kalman_update(series, misfit, prior_mean, prior_precision):
    trend_rows = trend_basis()
    trend_gram = jnp.dot(trend_rows.T, trend_rows, precision=lax.Precision.HIGHEST)
    projected = jnp.dot(trend_rows.T, series.astype(jnp.float32), precision=lax.Precision.HIGHEST)
    inverse_noise = 1.0 / (0.1 + misfit.astype(jnp.float32))
    matrix = [
        [
            trend_gram[row_at, column_at] * inverse_noise
            + (prior_precision[row_at] if row_at == column_at else 0.0)
            for column_at in range(4)
        ]
        for row_at in range(4)
    ]
    right_side = [
        prior_precision[row_at] * prior_mean[row_at] + projected[row_at] * inverse_noise
        for row_at in range(4)
    ]
    return jnp.stack(solve_small(matrix, right_side), axis=0)


def on_device(
    interferograms, pseudo_inverse, date_pairs, ref_pixel, band_width, prior_mean, prior_precision
):
    kernel_taps = filter_taps(band_width)
    slab_count = lax.axis_size("rows")
    image_count, local_rows, columns = interferograms.shape
    slab_cols = columns // slab_count
    smoothed = lax.optimization_barrier(column_pass(interferograms, kernel_taps))
    extended = padded_2(smoothed, (("rows", 1),), RADIUS)
    lowpass = row_pass(extended.astype(jnp.float32), kernel_taps, local_rows)
    filtered = (interferograms.astype(jnp.float32) - lowpass).astype(jnp.bfloat16)
    design = design_of(date_pairs)
    values = filtered.reshape(image_count, local_rows * columns)
    displacement = jnp.dot(pseudo_inverse, values, preferred_element_type=jnp.float32).astype(
        jnp.bfloat16
    )
    misfit = misfit_of(values, displacement, design)
    ref_index = ref_pixel[0]
    ref_row = ref_index // columns
    ref_col = ref_index % columns
    owner = ref_row // local_rows
    local_pixel = (ref_row - owner * local_rows) * columns + ref_col
    own_series = lax.dynamic_slice_in_dim(displacement, local_pixel, 1, 1)[:, 0]
    own_term = jnp.where(lax.axis_index("rows") == owner, own_series.astype(jnp.float32), 0.0)
    ref_series = lax.psum(own_term, "rows")
    packed = jnp.concatenate([displacement, misfit[None]], axis=0)
    packed = packed.reshape(DATES + 1, local_rows, columns)
    arrived = from_sources(
        lax.all_to_all(
            slab_major(packed, slab_count, slab_cols), "rows", split_axis=0, concat_axis=0, tiled=True
        )
    )
    slab_disp, slab_misfit = arrived[:DATES], arrived[DATES]
    series = (slab_disp.astype(jnp.float32) - ref_series[:, None]).astype(jnp.bfloat16)
    kalman_state = kalman_update(series, slab_misfit, prior_mean[0], prior_precision[0])
    return (series[None], kalman_state[None], slab_misfit[None])


def solution(mesh):
    placed = (
        P(None, ("frame", "rows"), None),
        P(),
        P(),
        P("frame"),
        P(),
        P(("frame", "rows"), None, None),
        P(("frame", "rows"), None, None),
    )
    return jax.shard_map(
        on_device,
        mesh=mesh,
        in_specs=placed,
        out_specs=(
            P(("frame", "rows"), None, None),
            P(("frame", "rows"), None, None),
            P(("frame", "rows"), None),
        ),
        check_vma=False,
    )
```

```python
import functools
import math

import jax
import jax.numpy as jnp
import ml_dtypes
import numpy as np
from jax import lax
from jax.experimental import pallas as pl
from jax.experimental.pallas import tpu as pltpu
from jax.sharding import PartitionSpec as P

DATES = 200
RADIUS = 4
MESH = pl.DeviceIdType.MESH


def padded_2(cells, sides, width):
    for axis, dim in sides:
        count = lax.axis_size(axis)
        ends = count - 1
        head = lax.slice_in_dim(cells, 0, width, axis=dim)
        tail = lax.slice_in_dim(cells, cells.shape[dim] - width, cells.shape[dim], axis=dim)
        cells = jnp.concatenate(
            [
                lax.ppermute(tail, axis, [(i, (i + 1) % count) for i in range(ends)]),
                cells,
                lax.ppermute(head, axis, [((i + 1) % count, i) for i in range(ends)]),
            ],
            axis=dim,
        )
    return cells


def filter_taps(band_width):
    spread = band_width[0].astype(jnp.float32) / 10.0
    offsets = jnp.arange(-RADIUS, RADIUS + 1).astype(jnp.float32)
    raw_taps = jnp.exp(-offsets * offsets / (2.0 * spread * spread))
    return raw_taps / jnp.sum(raw_taps)


def column_pass(images, kernel_taps):
    values = images.astype(jnp.float32)
    columns = values.shape[2]
    padded = jnp.pad(values, ((0, 0), (0, 0), (RADIUS, RADIUS)))
    summed = kernel_taps[0] * padded[:, :, 0:columns]
    for offset in range(1, 2 * RADIUS + 1):
        summed = summed + kernel_taps[offset] * padded[:, :, offset : offset + columns]
    return summed.astype(jnp.bfloat16)


def row_pass(extended, kernel_taps, height):
    summed = kernel_taps[0] * extended[:, 0:height]
    for offset in range(1, 2 * RADIUS + 1):
        summed = summed + kernel_taps[offset] * extended[:, offset : offset + height]
    return summed


def design_of(date_pairs):
    date_index = jnp.arange(DATES, dtype=jnp.int32)
    later_date = (date_index[None, :] == date_pairs[1][:, None]).astype(jnp.float32)
    earlier = (date_index[None, :] == date_pairs[0][:, None]).astype(jnp.float32)
    return (later_date - earlier).astype(jnp.bfloat16)


def trend_basis():
    epochs = jnp.arange(DATES).astype(jnp.float32)
    centred = (epochs - (DATES - 1) / 2.0) / DATES
    annual_phase = 2.0 * math.pi * 12.0 / 365.25 * epochs
    constant = jnp.ones_like(epochs)
    return jnp.stack([constant, centred, jnp.cos(annual_phase), jnp.sin(annual_phase)], axis=1)


def misfit_of(slab_values, displacement, design):
    modelled = jnp.dot(design, displacement, preferred_element_type=jnp.float32)
    residual = slab_values.astype(jnp.float32) - modelled
    return jnp.mean(residual * residual, axis=0).astype(jnp.bfloat16)


def slab_major(values, slab_count, slab_cols):
    leading, local_rows, columns = values.shape
    split_up = values.reshape(leading, local_rows, slab_count, slab_cols).transpose(2, 0, 1, 3)
    return split_up.reshape(slab_count, leading, local_rows * slab_cols)


def from_sources(arrived):
    sources, leading, piece_len = arrived.shape
    return arrived.transpose(1, 0, 2).reshape(leading, sources * piece_len)


def solve_small(matrix, right_side):
    dimension = len(right_side)
    factor = [[None] * dimension for row_at in range(dimension)]
    for column_at in range(dimension):
        pivot_sq = matrix[column_at][column_at]
        for term_at in range(column_at):
            pivot_sq = pivot_sq - factor[column_at][term_at] * factor[column_at][term_at]
        factor[column_at][column_at] = jnp.sqrt(pivot_sq)
        for row_at in range(column_at + 1, dimension):
            element = matrix[row_at][column_at]
            for term_at in range(column_at):
                element = element - factor[row_at][term_at] * factor[column_at][term_at]
            factor[row_at][column_at] = element / factor[column_at][column_at]
    forward = []
    for row_at in range(dimension):
        element = right_side[row_at]
        for term_at in range(row_at):
            element = element - factor[row_at][term_at] * forward[term_at]
        forward.append(element / factor[row_at][row_at])
    solution = [None] * dimension
    for row_at in reversed(range(dimension)):
        element = forward[row_at]
        for term_at in range(row_at + 1, dimension):
            element = element - factor[term_at][row_at] * solution[term_at]
        solution[row_at] = element / factor[row_at][row_at]
    return solution


def kalman_update(series, misfit, prior_mean, prior_precision):
    trend_rows = trend_basis()
    trend_gram = jnp.dot(trend_rows.T, trend_rows, precision=lax.Precision.HIGHEST)
    projected = jnp.dot(trend_rows.T, series.astype(jnp.float32), precision=lax.Precision.HIGHEST)
    inverse_noise = 1.0 / (0.1 + misfit.astype(jnp.float32))
    matrix = [
        [
            trend_gram[row_at, column_at] * inverse_noise
            + (prior_precision[row_at] if row_at == column_at else 0.0)
            for column_at in range(4)
        ]
        for row_at in range(4)
    ]
    right_side = [
        prior_precision[row_at] * prior_mean[row_at] + projected[row_at] * inverse_noise
        for row_at in range(4)
    ]
    return jnp.stack(solve_small(matrix, right_side), axis=0)


def in_steps(
    interferograms, pseudo_inverse, date_pairs, ref_pixel, band_width, prior_mean, prior_precision
):
    kernel_taps = filter_taps(band_width)
    slab_count = lax.axis_size("rows")
    image_count, local_rows, columns = interferograms.shape
    slab_cols = columns // slab_count
    smoothed = lax.optimization_barrier(column_pass(interferograms, kernel_taps))
    extended = padded_2(smoothed, (("rows", 1),), RADIUS)
    lowpass = row_pass(extended.astype(jnp.float32), kernel_taps, local_rows)
    filtered = (interferograms.astype(jnp.float32) - lowpass).astype(jnp.bfloat16)
    design = design_of(date_pairs)
    values = filtered.reshape(image_count, local_rows * columns)
    displacement = jnp.dot(pseudo_inverse, values, preferred_element_type=jnp.float32).astype(
        jnp.bfloat16
    )
    misfit = misfit_of(values, displacement, design)
    ref_index = ref_pixel[0]
    ref_row = ref_index // columns
    ref_col = ref_index % columns
    owner = ref_row // local_rows
    local_pixel = (ref_row - owner * local_rows) * columns + ref_col
    own_series = lax.dynamic_slice_in_dim(displacement, local_pixel, 1, 1)[:, 0]
    own_term = jnp.where(lax.axis_index("rows") == owner, own_series.astype(jnp.float32), 0.0)
    ref_series = lax.psum(own_term, "rows")
    packed = jnp.concatenate([displacement, misfit[None]], axis=0)
    packed = packed.reshape(DATES + 1, local_rows, columns)
    arrived = from_sources(
        lax.all_to_all(
            slab_major(packed, slab_count, slab_cols), "rows", split_axis=0, concat_axis=0, tiled=True
        )
    )
    slab_disp, slab_misfit = arrived[:DATES], arrived[DATES]
    series = (slab_disp.astype(jnp.float32) - ref_series[:, None]).astype(jnp.bfloat16)
    kalman_state = kalman_update(series, slab_misfit, prior_mean[0], prior_precision[0])
    return (series[None], kalman_state[None], slab_misfit[None])


PAD_IMAGES = 608
PAD_DEPTH = 640
PAD_DATES = 208
LANES = 128
HALVES = 2
RAISED = 56 * 1024 * 1024


def split_three(values):
    first = values.astype(jnp.bfloat16)
    rest = values - first.astype(jnp.float32)
    second = rest.astype(jnp.bfloat16)
    third = (rest - second.astype(jnp.float32)).astype(jnp.bfloat16)
    return first, second, third


def dot_f32(left, right):
    return jnp.dot(left, right, preferred_element_type=jnp.float32)


def iota(shape, dim):
    return lax.broadcasted_iota(jnp.int32, shape, dim)


def column_of(lane, half, slab_cols):
    return (HALVES * (lane // slab_cols) + half) * slab_cols + lane % slab_cols


def kernel(
    n,
    gram,
    ifg_ref,
    pinv_ref,
    pairs_ref,
    pixel_ref,
    band_ref,
    mean_ref,
    precision_ref,
    trend_ref,
    series_ref,
    state_ref,
    misfit_ref,
    by_row,
    weights,
    own,
    smooth,
    halo,
    filt,
    pinv_s,
    design_s,
    disp_s,
    sent,
    recv,
    ref_out,
    ref_in,
    proj,
    halo_send,
    halo_recv,
    part_send,
    part_recv,
    ref_send,
    ref_recv,
    self_sem,
):
    images, local_rows, columns = ifg_ref.shape
    slab_cols = columns // n
    per_half = n // HALVES
    me = lax.axis_index("rows")

    barrier = pltpu.get_barrier_semaphore()

    @pl.loop(1, n)
    def _(k):
        pl.semaphore_signal(barrier, inc=1, device_id={"rows": lax.rem(me + k, n)}, device_id_type=MESH)

    spread = jnp.full((8, LANES), band_ref[0], jnp.int32).astype(jnp.float32) / 10.0
    denominator = 2.0 * spread * spread
    raw = [jnp.exp(jnp.full((8, LANES), -float(k * k), jnp.float32) / denominator) for k in range(RADIUS + 1)]
    total = raw[0]
    for k in range(1, RADIUS + 1):
        total = total + 2.0 * raw[k]
    taps = [value / total for value in raw]
    lane = iota((columns, columns), 1)
    source = column_of(lane % LANES, lane // LANES, slab_cols)
    away = jnp.abs(iota((columns, columns), 0) - source)
    banded = jnp.zeros((columns, columns), jnp.float32)
    for k in range(RADIUS + 1):
        banded = jnp.where(away == k, taps[k][0:1, 0:1], banded)
    for at, piece in enumerate(split_three(banded)):
        weights[at] = piece
    weights[3] = jnp.where(away == 0, 1.0, 0.0).astype(jnp.bfloat16)

    size = 16 * local_rows
    out_at, in_at = iota((size, size), 0), iota((size, size), 1)
    order = jnp.where((out_at % 16) * local_rows + out_at // 16 == in_at, 1.0, 0.0).astype(jnp.bfloat16)

    def regroup(values, first):
        moved = dot_f32(order, values.astype(jnp.bfloat16)).astype(jnp.bfloat16)
        for r in range(local_rows):
            by_row[r, pl.ds(first, 16), :] = moved[r * 16 : (r + 1) * 16]

    whole = images // 16

    @pl.loop(0, whole, unroll=True)
    def _(g):
        first = pl.multiple_of(g * 16, 16)
        values = ifg_ref[pl.ds(first, 16)].astype(jnp.float32)
        regroup(values.reshape(size, columns), first)

    left_over = images - whole * 16
    if left_over:
        values = ifg_ref[whole * 16 :].astype(jnp.float32).reshape(left_over * local_rows, columns)
        regroup(
            jnp.concatenate([values, jnp.zeros((size - left_over * local_rows, columns), jnp.float32)], axis=0),
            whole * 16,
        )

    def smooth_row(r):
        values = by_row[r]
        made = dot_f32(values, weights[0]) + dot_f32(values, weights[1]) + dot_f32(values, weights[2])
        made = made.astype(jnp.bfloat16)
        for h in range(HALVES):
            smooth[h, r] = made[:, h * LANES : (h + 1) * LANES]

    def halo_copy(down, h):
        rows = pl.ds(local_rows - RADIUS, RADIUS) if down else pl.ds(0, RADIUS)
        side = 0 if down else 1
        to = jnp.minimum(me + 1, n - 1) if down else jnp.maximum(me - 1, 0)
        return pltpu.make_async_remote_copy(
            src_ref=smooth.at[h, rows],
            dst_ref=halo.at[side, h],
            send_sem=halo_send.at[side, h],
            recv_sem=halo_recv.at[side, h],
            device_id={"rows": to},
            device_id_type=MESH,
        )

    pl.loop(local_rows - RADIUS, local_rows)(smooth_row)
    pl.semaphore_wait(barrier, n - 1)

    @pl.when(me < n - 1)
    def _():
        halo_copy(True, 0).start()

    pl.loop(0, local_rows - RADIUS)(smooth_row)

    @pl.when(me > 0)
    def _():
        halo_copy(False, 0).start()

    @pl.when(me < n - 1)
    def _():
        halo_copy(True, 1).start()

    @pl.when(me > 0)
    def _():
        halo_copy(False, 1).start()

    @pl.loop(0, local_rows)
    def _(r):
        made = dot_f32(by_row[r], weights[3]).astype(jnp.bfloat16)
        for h in range(HALVES):
            own[h, r] = made[:, h * LANES : (h + 1) * LANES]

    @pl.when(me == 0)
    def _():
        halo[0] = jnp.zeros(halo.shape[1:], halo.dtype)

    @pl.when(me == n - 1)
    def _():
        halo[1] = jnp.zeros(halo.shape[1:], halo.dtype)

    pinv_s[...] = jnp.zeros_like(pinv_s)
    pinv_s[0:DATES, 0:images] = pinv_ref[...]
    date = iota((256, images), 0)
    later = jnp.where(date == pairs_ref[1:2, :], 1.0, 0.0)
    earlier = jnp.where(date == pairs_ref[0:1, :], 1.0, 0.0)
    both = jnp.concatenate([later - earlier, jnp.zeros((256, PAD_DEPTH - images), jnp.float32)], axis=1)
    design_s[...] = both.T.astype(jnp.bfloat16)
    filt[PAD_IMAGES:, :] = jnp.zeros((PAD_DEPTH - PAD_IMAGES, local_rows * LANES), jnp.bfloat16)

    pixel = pixel_ref[0]
    ref_row, ref_col = pixel // columns, pixel % columns
    ref_total = jnp.zeros((16, 256), jnp.float32)
    block_lanes = 256

    def part_copy(h, k):
        q = lax.rem(me // HALVES + k, per_half)
        return pltpu.make_async_remote_copy(
            src_ref=sent.at[h, q],
            dst_ref=recv.at[me],
            send_sem=part_send.at[h, k],
            recv_sem=part_recv.at[me],
            device_id={"rows": HALVES * q + h},
            device_id_type=MESH,
        )

    def ref_copy(k):
        return pltpu.make_async_remote_copy(
            src_ref=ref_out,
            dst_ref=ref_in.at[me],
            send_sem=ref_send.at[k],
            recv_sem=ref_recv.at[me],
            device_id={"rows": lax.rem(me + k, n)},
            device_id_type=MESH,
        )

    for h in range(HALVES):

        @pl.when(me > 0)
        def _():
            halo_copy(True, h).wait_recv()

        @pl.when(me < n - 1)
        def _():
            halo_copy(False, h).wait_recv()

        @pl.loop(0, PAD_IMAGES // 16)
        def _(g):
            block = pl.ds(pl.multiple_of(g * 16, 16), 16)
            lines = [halo[0, h, t, block, :] for t in range(RADIUS)]
            lines += [smooth[h, r, block, :] for r in range(local_rows)]
            lines += [halo[1, h, t, block, :] for t in range(RADIUS)]
            lines = [line.astype(jnp.float32) for line in lines]
            for r in range(local_rows):
                low = lines[r + RADIUS] * taps[0][0:1]
                for k in range(1, RADIUS + 1):
                    low = low + (lines[r + RADIUS - k] + lines[r + RADIUS + k]) * taps[k][0:1]
                high = own[h, r, block, :].astype(jnp.float32) - low
                filt[block, r * LANES : (r + 1) * LANES] = high.astype(jnp.bfloat16)

        for b in range(local_rows * LANES // block_lanes):
            lanes = slice(b * block_lanes, (b + 1) * block_lanes)
            values = filt[:, lanes]
            disp = dot_f32(pinv_s[...], values).astype(jnp.bfloat16)
            disp_wide = jnp.concatenate([disp, jnp.zeros((256 - PAD_DATES, block_lanes), jnp.bfloat16)], axis=0)
            residual = values.astype(jnp.float32) - dot_f32(design_s[...], disp_wide)
            misfit = jnp.sum(residual * residual, axis=0, keepdims=True) / images
            at = iota((16, block_lanes), 1) + b * block_lanes
            hit = (at // LANES + me * local_rows == ref_row) & (column_of(at % LANES, h, slab_cols) == ref_col)
            ref_total += lax.dot_general(
                jnp.where(hit, 1.0, 0.0).astype(jnp.bfloat16),
                disp_wide,
                (((1,), (1,)), ((), ())),
                preferred_element_type=jnp.float32,
            )
            disp_s[0:DATES, lanes] = disp[0:DATES].astype(jnp.float32)
            disp_s[DATES:, lanes] = jnp.broadcast_to(misfit, (PAD_DATES - DATES, block_lanes))

        if h == HALVES - 1:
            ref_out[...] = ref_total.astype(jnp.bfloat16)

            @pl.loop(1, n)
            def _(k):
                ref_copy(k).start()

        @pl.loop(0, PAD_DATES // 16)
        def _(g):
            block = pl.ds(pl.multiple_of(g * 16, 16), 16)
            lines = [disp_s[block, r * LANES : (r + 1) * LANES] for r in range(local_rows)]
            place = iota((16, LANES), 1) // slab_cols
            for q in range(per_half):
                made = None
                for r in range(local_rows):
                    shift = ((r - q) * slab_cols) % LANES
                    moved = pltpu.roll(lines[r], shift, 1) if shift else lines[r]
                    made = moved if made is None else jnp.where(place == r, moved, made)
                sent[h, q, block, :] = made.astype(jnp.bfloat16)

        @pl.when(me % HALVES == h)
        def _():
            local = pltpu.make_async_copy(sent.at[h, me // HALVES], recv.at[me], self_sem)
            local.start()
            local.wait()

        @pl.when(me % HALVES != h)
        def _():
            part_copy(h, 0).start()

        @pl.loop(1, per_half)
        def _(k):
            part_copy(h, k).start()

    @pl.loop(1, n)
    def _(k):
        j = lax.rem(me + k, n)
        pltpu.make_async_remote_copy(
            src_ref=ref_out,
            dst_ref=ref_in.at[j],
            send_sem=ref_send.at[k],
            recv_sem=ref_recv.at[j],
            device_id={"rows": j},
            device_id_type=MESH,
        ).wait_recv()

    ref_in[me] = ref_out[...]
    ref_sum = ref_in[0].astype(jnp.float32)
    for j in range(1, n):
        ref_sum = ref_sum + ref_in[j].astype(jnp.float32)
    ref_column = jnp.broadcast_to(ref_sum[0:1], (LANES, 256)).T[0:PAD_DATES]

    @pl.loop(0, n)
    def _(k):
        j = lax.rem(me + k, n)

        @pl.when(k > 0)
        def _():
            pltpu.make_async_remote_copy(
                src_ref=sent.at[0, 0],
                dst_ref=recv.at[j],
                send_sem=part_send.at[0, 0],
                recv_sem=part_recv.at[j],
                device_id={"rows": j},
                device_id_type=MESH,
            ).wait_recv()

        values = recv[j].astype(jnp.float32)
        lanes = pl.ds(pl.multiple_of(j * LANES, LANES), LANES)
        series = (values - ref_column).astype(jnp.bfloat16)
        series_ref[0, :, lanes] = series[0:DATES]
        made = dot_f32(trend_ref[...], series)
        proj[0:4, lanes] = made[0:4] + (made[4:8] + made[8:12])
        proj[4:5, lanes] = values[DATES : DATES + 1]

    misfit = proj[4:5, :]
    misfit_ref[...] = misfit.astype(jnp.bfloat16)
    inverse_noise = 1.0 / (0.1 + misfit)
    precision = [precision_ref[0, d : d + 1, :] for d in range(4)]
    matrix = [
        [float(gram[a][b]) * inverse_noise + (precision[a] if a == b else 0.0) for b in range(4)]
        for a in range(4)
    ]
    right_side = [precision[d] * mean_ref[0, d : d + 1, :] + proj[d : d + 1, :] * inverse_noise for d in range(4)]
    for d, value in enumerate(solve_small(matrix, right_side)):
        state_ref[0, d : d + 1, :] = value

    for h in range(HALVES):

        @pl.when(me < n - 1)
        def _():
            halo_copy(True, h).wait_send()

        @pl.when(me > 0)
        def _():
            halo_copy(False, h).wait_send()

        @pl.when(me % HALVES != h)
        def _():
            part_copy(h, 0).wait_send()

        @pl.loop(1, per_half)
        def _(k):
            part_copy(h, k).wait_send()

    @pl.loop(1, n)
    def _(k):
        ref_copy(k).wait_send()


def trend_constants():
    epochs = np.arange(DATES, dtype=np.float64)
    phase = 2.0 * np.pi * 12.0 / 365.25 * epochs
    rows = np.stack([np.ones_like(epochs), (epochs - (DATES - 1) / 2.0) / DATES, np.cos(phase), np.sin(phase)])
    return rows.astype(np.float32)


def in_kernel(interferograms, pseudo_inverse, date_pairs, ref_pixel, band_width, prior_mean, prior_precision):
    n = lax.axis_size("rows")
    images, local_rows, columns = interferograms.shape
    rows = trend_constants()
    gram = (rows.astype(np.float64) @ rows.astype(np.float64).T).astype(np.float32)
    pieces, rest = [], rows
    for _ in range(3):
        piece = rest.astype(ml_dtypes.bfloat16)
        pieces.append(piece)
        rest = rest - piece.astype(np.float32)
    trend = np.zeros((16, PAD_DATES), ml_dtypes.bfloat16)
    trend[0:12, 0:DATES] = np.concatenate(pieces, axis=0)
    vmem, smem = pl.BlockSpec(memory_space=pltpu.VMEM), pl.BlockSpec(memory_space=pltpu.SMEM)
    half_rows = (HALVES, local_rows, PAD_IMAGES, LANES)
    bf16, f32 = jnp.bfloat16, jnp.float32
    per_half = n // HALVES
    dma = pltpu.SemaphoreType.DMA
    return pl.pallas_call(
        functools.partial(kernel, n, gram.tolist()),
        out_shape=(
            jax.ShapeDtypeStruct((1, DATES, n * LANES), bf16),
            jax.ShapeDtypeStruct((1, 4, n * LANES), f32),
            jax.ShapeDtypeStruct((1, n * LANES), bf16),
        ),
        in_specs=[vmem, vmem, vmem, smem, smem, vmem, vmem, vmem],
        out_specs=(vmem, vmem, vmem),
        scratch_shapes=[
            pltpu.VMEM((local_rows, PAD_IMAGES, columns), bf16),
            pltpu.VMEM((4, columns, columns), bf16),
            pltpu.VMEM(half_rows, bf16),
            pltpu.VMEM(half_rows, bf16),
            pltpu.VMEM((2, HALVES, RADIUS, PAD_IMAGES, LANES), bf16),
            pltpu.VMEM((PAD_DEPTH, local_rows * LANES), bf16),
            pltpu.VMEM((PAD_DATES, PAD_DEPTH), bf16),
            pltpu.VMEM((PAD_DEPTH, 256), bf16),
            pltpu.VMEM((PAD_DATES, local_rows * LANES), f32),
            pltpu.VMEM((HALVES, per_half, PAD_DATES, LANES), bf16),
            pltpu.VMEM((n, PAD_DATES, LANES), bf16),
            pltpu.VMEM((16, 256), bf16),
            pltpu.VMEM((n, 16, 256), bf16),
            pltpu.VMEM((8, n * LANES), f32),
            dma((2, HALVES)),
            dma((2, HALVES)),
            dma((HALVES, per_half)),
            dma((n,)),
            dma((n,)),
            dma((n,)),
            dma,
        ],
        compiler_params=pltpu.CompilerParams(
            collective_id=0, has_side_effects=True, vmem_limit_bytes=RAISED
        ),
    )(
        interferograms,
        pseudo_inverse,
        date_pairs,
        ref_pixel,
        band_width,
        prior_mean,
        prior_precision,
        jnp.asarray(trend),
    )


def on_device(
    interferograms, pseudo_inverse, date_pairs, ref_pixel, band_width, prior_mean, prior_precision
):
    n = lax.axis_size("rows")
    images, local_rows, columns = interferograms.shape
    fits = (columns // n) * local_rows == LANES and columns == HALVES * LANES and n % HALVES == 0
    fits = fits and local_rows == 2 * RADIUS and images == 600
    chosen = in_kernel if fits else in_steps
    return chosen(
        interferograms, pseudo_inverse, date_pairs, ref_pixel, band_width, prior_mean, prior_precision
    )


def solution(mesh):
    placed = (
        P(None, ("frame", "rows"), None),
        P(),
        P(),
        P("frame"),
        P(),
        P(("frame", "rows"), None, None),
        P(("frame", "rows"), None, None),
    )
    return jax.shard_map(
        on_device,
        mesh=mesh,
        in_specs=placed,
        out_specs=(
            P(("frame", "rows"), None, None),
            P(("frame", "rows"), None, None),
            P(("frame", "rows"), None),
        ),
        check_vma=False,
    )
```

```python
import functools
import math

import jax
import jax.numpy as jnp
import ml_dtypes
import numpy as np
from jax import lax
from jax.experimental import pallas as pl
from jax.experimental.pallas import tpu as pltpu
from jax.sharding import PartitionSpec as P

DATES = 200
RADIUS = 4
MESH = pl.DeviceIdType.MESH


def padded_2(cells, sides, width):
    for axis, dim in sides:
        count = lax.axis_size(axis)
        ends = count - 1
        head = lax.slice_in_dim(cells, 0, width, axis=dim)
        tail = lax.slice_in_dim(cells, cells.shape[dim] - width, cells.shape[dim], axis=dim)
        cells = jnp.concatenate(
            [
                lax.ppermute(tail, axis, [(i, (i + 1) % count) for i in range(ends)]),
                cells,
                lax.ppermute(head, axis, [((i + 1) % count, i) for i in range(ends)]),
            ],
            axis=dim,
        )
    return cells


def filter_taps(band_width):
    spread = band_width[0].astype(jnp.float32) / 10.0
    offsets = jnp.arange(-RADIUS, RADIUS + 1).astype(jnp.float32)
    raw_taps = jnp.exp(-offsets * offsets / (2.0 * spread * spread))
    return raw_taps / jnp.sum(raw_taps)


def column_pass(images, kernel_taps):
    values = images.astype(jnp.float32)
    columns = values.shape[2]
    padded = jnp.pad(values, ((0, 0), (0, 0), (RADIUS, RADIUS)))
    summed = kernel_taps[0] * padded[:, :, 0:columns]
    for offset in range(1, 2 * RADIUS + 1):
        summed = summed + kernel_taps[offset] * padded[:, :, offset : offset + columns]
    return summed.astype(jnp.bfloat16)


def row_pass(extended, kernel_taps, height):
    summed = kernel_taps[0] * extended[:, 0:height]
    for offset in range(1, 2 * RADIUS + 1):
        summed = summed + kernel_taps[offset] * extended[:, offset : offset + height]
    return summed


def design_of(date_pairs):
    date_index = jnp.arange(DATES, dtype=jnp.int32)
    later_date = (date_index[None, :] == date_pairs[1][:, None]).astype(jnp.float32)
    earlier = (date_index[None, :] == date_pairs[0][:, None]).astype(jnp.float32)
    return (later_date - earlier).astype(jnp.bfloat16)


def trend_basis():
    epochs = jnp.arange(DATES).astype(jnp.float32)
    centred = (epochs - (DATES - 1) / 2.0) / DATES
    annual_phase = 2.0 * math.pi * 12.0 / 365.25 * epochs
    constant = jnp.ones_like(epochs)
    return jnp.stack([constant, centred, jnp.cos(annual_phase), jnp.sin(annual_phase)], axis=1)


def misfit_of(slab_values, displacement, design):
    modelled = jnp.dot(design, displacement, preferred_element_type=jnp.float32)
    residual = slab_values.astype(jnp.float32) - modelled
    return jnp.mean(residual * residual, axis=0).astype(jnp.bfloat16)


def slab_major(values, slab_count, slab_cols):
    leading, local_rows, columns = values.shape
    split_up = values.reshape(leading, local_rows, slab_count, slab_cols).transpose(2, 0, 1, 3)
    return split_up.reshape(slab_count, leading, local_rows * slab_cols)


def from_sources(arrived):
    sources, leading, piece_len = arrived.shape
    return arrived.transpose(1, 0, 2).reshape(leading, sources * piece_len)


def solve_small(matrix, right_side):
    dimension = len(right_side)
    factor = [[None] * dimension for row_at in range(dimension)]
    for column_at in range(dimension):
        pivot_sq = matrix[column_at][column_at]
        for term_at in range(column_at):
            pivot_sq = pivot_sq - factor[column_at][term_at] * factor[column_at][term_at]
        factor[column_at][column_at] = jnp.sqrt(pivot_sq)
        for row_at in range(column_at + 1, dimension):
            element = matrix[row_at][column_at]
            for term_at in range(column_at):
                element = element - factor[row_at][term_at] * factor[column_at][term_at]
            factor[row_at][column_at] = element / factor[column_at][column_at]
    forward = []
    for row_at in range(dimension):
        element = right_side[row_at]
        for term_at in range(row_at):
            element = element - factor[row_at][term_at] * forward[term_at]
        forward.append(element / factor[row_at][row_at])
    solution = [None] * dimension
    for row_at in reversed(range(dimension)):
        element = forward[row_at]
        for term_at in range(row_at + 1, dimension):
            element = element - factor[term_at][row_at] * solution[term_at]
        solution[row_at] = element / factor[row_at][row_at]
    return solution


def kalman_update(series, misfit, prior_mean, prior_precision):
    trend_rows = trend_basis()
    trend_gram = jnp.dot(trend_rows.T, trend_rows, precision=lax.Precision.HIGHEST)
    projected = jnp.dot(trend_rows.T, series.astype(jnp.float32), precision=lax.Precision.HIGHEST)
    inverse_noise = 1.0 / (0.1 + misfit.astype(jnp.float32))
    matrix = [
        [
            trend_gram[row_at, column_at] * inverse_noise
            + (prior_precision[row_at] if row_at == column_at else 0.0)
            for column_at in range(4)
        ]
        for row_at in range(4)
    ]
    right_side = [
        prior_precision[row_at] * prior_mean[row_at] + projected[row_at] * inverse_noise
        for row_at in range(4)
    ]
    return jnp.stack(solve_small(matrix, right_side), axis=0)


def in_steps(
    interferograms, pseudo_inverse, date_pairs, ref_pixel, band_width, prior_mean, prior_precision
):
    kernel_taps = filter_taps(band_width)
    slab_count = lax.axis_size("rows")
    image_count, local_rows, columns = interferograms.shape
    slab_cols = columns // slab_count
    smoothed = lax.optimization_barrier(column_pass(interferograms, kernel_taps))
    extended = padded_2(smoothed, (("rows", 1),), RADIUS)
    lowpass = row_pass(extended.astype(jnp.float32), kernel_taps, local_rows)
    filtered = (interferograms.astype(jnp.float32) - lowpass).astype(jnp.bfloat16)
    design = design_of(date_pairs)
    values = filtered.reshape(image_count, local_rows * columns)
    displacement = jnp.dot(pseudo_inverse, values, preferred_element_type=jnp.float32).astype(
        jnp.bfloat16
    )
    misfit = misfit_of(values, displacement, design)
    ref_index = ref_pixel[0]
    ref_row = ref_index // columns
    ref_col = ref_index % columns
    owner = ref_row // local_rows
    local_pixel = (ref_row - owner * local_rows) * columns + ref_col
    own_series = lax.dynamic_slice_in_dim(displacement, local_pixel, 1, 1)[:, 0]
    own_term = jnp.where(lax.axis_index("rows") == owner, own_series.astype(jnp.float32), 0.0)
    ref_series = lax.psum(own_term, "rows")
    packed = jnp.concatenate([displacement, misfit[None]], axis=0)
    packed = packed.reshape(DATES + 1, local_rows, columns)
    arrived = from_sources(
        lax.all_to_all(
            slab_major(packed, slab_count, slab_cols), "rows", split_axis=0, concat_axis=0, tiled=True
        )
    )
    slab_disp, slab_misfit = arrived[:DATES], arrived[DATES]
    series = (slab_disp.astype(jnp.float32) - ref_series[:, None]).astype(jnp.bfloat16)
    kalman_state = kalman_update(series, slab_misfit, prior_mean[0], prior_precision[0])
    return (series[None], kalman_state[None], slab_misfit[None])


PAD_IMAGES = 608
PAD_DEPTH = 640
PAD_DATES = 208
LANES = 128
GROUP = 32
UNROLL = True
HALVES = 2
RAISED = 56 * 1024 * 1024


def split_three(values):
    first = values.astype(jnp.bfloat16)
    rest = values - first.astype(jnp.float32)
    second = rest.astype(jnp.bfloat16)
    third = (rest - second.astype(jnp.float32)).astype(jnp.bfloat16)
    return first, second, third


def dot_f32(left, right):
    return jnp.dot(left, right, preferred_element_type=jnp.float32)


def iota(shape, dim):
    return lax.broadcasted_iota(jnp.int32, shape, dim)


def column_of(lane, half, slab_cols):
    return (HALVES * (lane // slab_cols) + half) * slab_cols + lane % slab_cols


def kernel(
    n,
    ifg_ref,
    pinv_ref,
    pairs_ref,
    pixel_ref,
    band_ref,
    recv,
    ref_sum,
    by_row,
    weights,
    own,
    smooth,
    halo,
    filt,
    pinv_s,
    design_s,
    disp_s,
    sent,
    ref_out,
    ref_in,
    round_sem,
    halo_send,
    halo_recv,
    part_send,
    part_recv,
    ref_send,
    ref_recv,
    self_sem,
):
    local_rows, columns = filt.shape[1] // LANES, ifg_ref.shape[1]
    images = ifg_ref.shape[0] // local_rows
    slab_cols = columns // n
    per_half = n // HALVES
    me = lax.axis_index("rows")

    barrier = pltpu.get_barrier_semaphore()

    partners = [lax.rem(me + away, n) for away in (1, n - 1, 4, n - 4)]

    def greet(semaphore):
        for partner in partners:
            pl.semaphore_signal(semaphore, inc=1, device_id={"rows": partner}, device_id_type=MESH)

    greet(barrier)

    spread = jnp.full((8, LANES), band_ref[0], jnp.int32).astype(jnp.float32) / 10.0
    denominator = 2.0 * spread * spread
    raw = [jnp.exp(jnp.full((8, LANES), -float(k * k), jnp.float32) / denominator) for k in range(RADIUS + 1)]
    total = raw[0]
    for k in range(1, RADIUS + 1):
        total = total + 2.0 * raw[k]
    taps = [value / total for value in raw]
    lane = iota((columns, columns), 1)
    source = column_of(lane % LANES, lane // LANES, slab_cols)
    away = jnp.abs(iota((columns, columns), 0) - source)
    banded = jnp.zeros((columns, columns), jnp.float32)
    for k in range(RADIUS + 1):
        banded = jnp.where(away == k, taps[k][0:1, 0:1], banded)
    for at, piece in enumerate(split_three(banded)):
        weights[at] = piece
    weights[3] = jnp.where(away == 0, 1.0, 0.0).astype(jnp.bfloat16)

    size = GROUP * local_rows
    out_at, in_at = iota((size, size), 0), iota((size, size), 1)
    order = jnp.where((out_at % GROUP) * local_rows + out_at // GROUP == in_at, 1.0, 0.0).astype(jnp.bfloat16)

    def regroup(values, first):
        moved = dot_f32(order, values).astype(jnp.bfloat16)
        for r in range(local_rows):
            by_row[r, pl.ds(first, GROUP), :] = moved[r * GROUP : (r + 1) * GROUP]

    whole = images // GROUP

    @pl.loop(0, whole, unroll=UNROLL)
    def _(g):
        regroup(ifg_ref[pl.ds(pl.multiple_of(g * size, size), size), :], pl.multiple_of(g * GROUP, GROUP))

    left_over = images * local_rows - whole * size
    if left_over:
        values = ifg_ref[whole * size :, :]
        regroup(
            jnp.concatenate([values, jnp.zeros((size - left_over, columns), jnp.bfloat16)], axis=0),
            whole * GROUP,
        )

    def smooth_row(r):
        values = by_row[r]
        made = dot_f32(values, weights[0]) + dot_f32(values, weights[1]) + dot_f32(values, weights[2])
        made = made.astype(jnp.bfloat16)
        for h in range(HALVES):
            smooth[h, r] = made[:, h * LANES : (h + 1) * LANES]

    def halo_copy(down, h):
        rows = pl.ds(local_rows - RADIUS, RADIUS) if down else pl.ds(0, RADIUS)
        side = 0 if down else 1
        to = jnp.minimum(me + 1, n - 1) if down else jnp.maximum(me - 1, 0)
        return pltpu.make_async_remote_copy(
            src_ref=smooth.at[h, rows],
            dst_ref=halo.at[side, h],
            send_sem=halo_send.at[side, h],
            recv_sem=halo_recv.at[side, h],
            device_id={"rows": to},
            device_id_type=MESH,
        )

    pl.loop(local_rows - RADIUS, local_rows)(smooth_row)
    pl.semaphore_wait(barrier, len(partners))

    @pl.when(me < n - 1)
    def _():
        halo_copy(True, 0).start()

    pl.loop(0, local_rows - RADIUS)(smooth_row)

    @pl.when(me > 0)
    def _():
        halo_copy(False, 0).start()

    @pl.when(me < n - 1)
    def _():
        halo_copy(True, 1).start()

    @pl.when(me > 0)
    def _():
        halo_copy(False, 1).start()

    greet(round_sem.at[0])

    @pl.loop(0, local_rows)
    def _(r):
        made = dot_f32(by_row[r], weights[3]).astype(jnp.bfloat16)
        for h in range(HALVES):
            own[h, r] = made[:, h * LANES : (h + 1) * LANES]

    @pl.when(me == 0)
    def _():
        halo[0] = jnp.zeros(halo.shape[1:], halo.dtype)

    @pl.when(me == n - 1)
    def _():
        halo[1] = jnp.zeros(halo.shape[1:], halo.dtype)

    pl.semaphore_wait(round_sem.at[0], len(partners))
    greet(round_sem.at[1])

    pinv_s[...] = jnp.zeros_like(pinv_s)
    pinv_s[0:DATES, 0:images] = pinv_ref[...]
    date = iota((256, images), 0)
    later = jnp.where(date == pairs_ref[1:2, :], 1.0, 0.0)
    earlier = jnp.where(date == pairs_ref[0:1, :], 1.0, 0.0)
    both = jnp.concatenate([later - earlier, jnp.zeros((256, PAD_DEPTH - images), jnp.float32)], axis=1)
    design_s[...] = both.T.astype(jnp.bfloat16)
    filt[PAD_IMAGES:, :] = jnp.zeros((PAD_DEPTH - PAD_IMAGES, local_rows * LANES), jnp.bfloat16)

    pl.semaphore_wait(round_sem.at[1], len(partners))
    pixel = pixel_ref[0]
    ref_row, ref_col = pixel // columns, pixel % columns
    ref_total = jnp.zeros((16, 256), jnp.float32)
    block_lanes = 256

    def part_copy(h, k):
        q = lax.rem(me // HALVES + k, per_half)
        return pltpu.make_async_remote_copy(
            src_ref=sent.at[h, q],
            dst_ref=recv.at[me],
            send_sem=part_send.at[h, k],
            recv_sem=part_recv.at[me],
            device_id={"rows": HALVES * q + h},
            device_id_type=MESH,
        )

    def ref_copy(k):
        return pltpu.make_async_remote_copy(
            src_ref=ref_out,
            dst_ref=ref_in.at[me],
            send_sem=ref_send.at[k],
            recv_sem=ref_recv.at[me],
            device_id={"rows": lax.rem(me + k, n)},
            device_id_type=MESH,
        )

    for h in range(HALVES):

        @pl.when(me > 0)
        def _():
            halo_copy(True, h).wait_recv()

        @pl.when(me < n - 1)
        def _():
            halo_copy(False, h).wait_recv()

        @pl.loop(0, PAD_IMAGES // 16)
        def _(g):
            block = pl.ds(pl.multiple_of(g * 16, 16), 16)
            lines = [halo[0, h, t, block, :] for t in range(RADIUS)]
            lines += [smooth[h, r, block, :] for r in range(local_rows)]
            lines += [halo[1, h, t, block, :] for t in range(RADIUS)]
            lines = [line.astype(jnp.float32) for line in lines]
            for r in range(local_rows):
                low = lines[r + RADIUS] * taps[0][0:1]
                for k in range(1, RADIUS + 1):
                    low = low + (lines[r + RADIUS - k] + lines[r + RADIUS + k]) * taps[k][0:1]
                high = own[h, r, block, :].astype(jnp.float32) - low
                filt[block, r * LANES : (r + 1) * LANES] = high.astype(jnp.bfloat16)

        for b in range(local_rows * LANES // block_lanes):
            lanes = slice(b * block_lanes, (b + 1) * block_lanes)
            values = filt[:, lanes]
            disp = dot_f32(pinv_s[...], values).astype(jnp.bfloat16)
            disp_wide = jnp.concatenate([disp, jnp.zeros((256 - PAD_DATES, block_lanes), jnp.bfloat16)], axis=0)
            residual = values.astype(jnp.float32) - dot_f32(design_s[...], disp_wide)
            misfit = jnp.sum(residual * residual, axis=0, keepdims=True) / images
            at = iota((16, block_lanes), 1) + b * block_lanes
            hit = (at // LANES + me * local_rows == ref_row) & (column_of(at % LANES, h, slab_cols) == ref_col)
            ref_total += lax.dot_general(
                jnp.where(hit, 1.0, 0.0).astype(jnp.bfloat16),
                disp_wide,
                (((1,), (1,)), ((), ())),
                preferred_element_type=jnp.float32,
            )
            disp_s[0:DATES, lanes] = disp[0:DATES].astype(jnp.float32)
            disp_s[DATES:, lanes] = jnp.broadcast_to(misfit, (PAD_DATES - DATES, block_lanes))

        if h == HALVES - 1:
            ref_out[...] = ref_total.astype(jnp.bfloat16)

            @pl.loop(1, n)
            def _(k):
                ref_copy(k).start()

        @pl.loop(0, PAD_DATES // 16)
        def _(g):
            block = pl.ds(pl.multiple_of(g * 16, 16), 16)
            lines = [disp_s[block, r * LANES : (r + 1) * LANES] for r in range(local_rows)]
            place = iota((16, LANES), 1) // slab_cols
            for q in range(per_half):
                made = None
                for r in range(local_rows):
                    shift = ((r - q) * slab_cols) % LANES
                    moved = pltpu.roll(lines[r], shift, 1) if shift else lines[r]
                    made = moved if made is None else jnp.where(place == r, moved, made)
                sent[h, q, block, :] = made.astype(jnp.bfloat16)

        @pl.when(me % HALVES == h)
        def _():
            local = pltpu.make_async_copy(sent.at[h, me // HALVES], recv.at[me], self_sem)
            local.start()
            local.wait()

        @pl.when(me % HALVES != h)
        def _():
            part_copy(h, 0).start()

        @pl.loop(1, per_half)
        def _(k):
            part_copy(h, k).start()

    @pl.loop(1, n)
    def _(k):
        j = lax.rem(me + k, n)
        pltpu.make_async_remote_copy(
            src_ref=ref_out,
            dst_ref=ref_in.at[j],
            send_sem=ref_send.at[k],
            recv_sem=ref_recv.at[j],
            device_id={"rows": j},
            device_id_type=MESH,
        ).wait_recv()

    ref_in[me] = ref_out[...]
    total = ref_in[0].astype(jnp.float32)
    for j in range(1, n):
        total = total + ref_in[j].astype(jnp.float32)
    ref_sum[...] = total

    @pl.loop(1, n)
    def _(k):
        j = lax.rem(me + k, n)
        pltpu.make_async_remote_copy(
            src_ref=sent.at[0, 0],
            dst_ref=recv.at[j],
            send_sem=part_send.at[0, 0],
            recv_sem=part_recv.at[j],
            device_id={"rows": j},
            device_id_type=MESH,
        ).wait_recv()

    for h in range(HALVES):

        @pl.when(me < n - 1)
        def _():
            halo_copy(True, h).wait_send()

        @pl.when(me > 0)
        def _():
            halo_copy(False, h).wait_send()

        @pl.when(me % HALVES != h)
        def _():
            part_copy(h, 0).wait_send()

        @pl.loop(1, per_half)
        def _(k):
            part_copy(h, k).wait_send()

    @pl.loop(1, n)
    def _(k):
        ref_copy(k).wait_send()


def finish(n, gram, arrived, ref_sum, mean_ref, precision_ref, trend_ref, series_ref, state_ref, misfit_ref, proj):
    ref_column = jnp.broadcast_to(ref_sum[0:1], (LANES, 256)).T[0:PAD_DATES]
    for j in range(n):
        values = arrived[j].astype(jnp.float32)
        lanes = slice(j * LANES, (j + 1) * LANES)
        series = (values - ref_column).astype(jnp.bfloat16)
        series_ref[0, :, lanes] = series[0:DATES]
        made = dot_f32(trend_ref[...], series)
        proj[0:4, lanes] = made[0:4] + (made[4:8] + made[8:12])
        proj[4:5, lanes] = values[DATES : DATES + 1]

    misfit = proj[4:5, :]
    misfit_ref[...] = misfit.astype(jnp.bfloat16)
    inverse_noise = 1.0 / (0.1 + misfit)
    precision = [precision_ref[0, d : d + 1, :] for d in range(4)]
    matrix = [
        [float(gram[a][b]) * inverse_noise + (precision[a] if a == b else 0.0) for b in range(4)]
        for a in range(4)
    ]
    right_side = [precision[d] * mean_ref[0, d : d + 1, :] + proj[d : d + 1, :] * inverse_noise for d in range(4)]
    for d, value in enumerate(solve_small(matrix, right_side)):
        state_ref[0, d : d + 1, :] = value


def trend_constants():
    epochs = np.arange(DATES, dtype=np.float64)
    phase = 2.0 * np.pi * 12.0 / 365.25 * epochs
    rows = np.stack([np.ones_like(epochs), (epochs - (DATES - 1) / 2.0) / DATES, np.cos(phase), np.sin(phase)])
    return rows.astype(np.float32)


def in_kernel(interferograms, pseudo_inverse, date_pairs, ref_pixel, band_width, prior_mean, prior_precision):
    n = lax.axis_size("rows")
    images, local_rows, columns = interferograms.shape
    rows = trend_constants()
    gram = (rows.astype(np.float64) @ rows.astype(np.float64).T).astype(np.float32)
    pieces, rest = [], rows
    for _ in range(3):
        piece = rest.astype(ml_dtypes.bfloat16)
        pieces.append(piece)
        rest = rest - piece.astype(np.float32)
    trend = np.zeros((16, PAD_DATES), ml_dtypes.bfloat16)
    trend[0:12, 0:DATES] = np.concatenate(pieces, axis=0)
    vmem, smem = pl.BlockSpec(memory_space=pltpu.VMEM), pl.BlockSpec(memory_space=pltpu.SMEM)
    half_rows = (HALVES, local_rows, PAD_IMAGES, LANES)
    bf16, f32 = jnp.bfloat16, jnp.float32
    per_half = n // HALVES
    dma = pltpu.SemaphoreType.DMA
    arrived, ref_sum = pl.pallas_call(
        functools.partial(kernel, n),
        out_shape=(
            jax.ShapeDtypeStruct((n, PAD_DATES, LANES), bf16),
            jax.ShapeDtypeStruct((16, 256), f32),
        ),
        in_specs=[vmem, vmem, vmem, smem, smem],
        out_specs=(pl.BlockSpec(memory_space=pl.ANY), vmem),
        scratch_shapes=[
            pltpu.VMEM((local_rows, PAD_IMAGES, columns), bf16),
            pltpu.VMEM((4, columns, columns), bf16),
            pltpu.VMEM(half_rows, bf16),
            pltpu.VMEM(half_rows, bf16),
            pltpu.VMEM((2, HALVES, RADIUS, PAD_IMAGES, LANES), bf16),
            pltpu.VMEM((PAD_DEPTH, local_rows * LANES), bf16),
            pltpu.VMEM((PAD_DATES, PAD_DEPTH), bf16),
            pltpu.VMEM((PAD_DEPTH, 256), bf16),
            pltpu.VMEM((PAD_DATES, local_rows * LANES), f32),
            pltpu.VMEM((HALVES, per_half, PAD_DATES, LANES), bf16),
            pltpu.VMEM((16, 256), bf16),
            pltpu.VMEM((n, 16, 256), bf16),
            pltpu.SemaphoreType.REGULAR((2,)),
            dma((2, HALVES)),
            dma((2, HALVES)),
            dma((HALVES, per_half)),
            dma((n,)),
            dma((n,)),
            dma((n,)),
            dma,
        ],
        compiler_params=pltpu.CompilerParams(
            collective_id=0, has_side_effects=True, vmem_limit_bytes=RAISED
        ),
    )(
        interferograms.reshape(images * local_rows, columns),
        pseudo_inverse,
        date_pairs,
        ref_pixel,
        band_width,
    )
    return pl.pallas_call(
        functools.partial(finish, n, gram.tolist()),
        out_shape=(
            jax.ShapeDtypeStruct((1, DATES, n * LANES), bf16),
            jax.ShapeDtypeStruct((1, 4, n * LANES), f32),
            jax.ShapeDtypeStruct((1, n * LANES), bf16),
        ),
        in_specs=[vmem] * 5,
        out_specs=(vmem, vmem, vmem),
        scratch_shapes=[pltpu.VMEM((8, n * LANES), f32)],
        compiler_params=pltpu.CompilerParams(vmem_limit_bytes=RAISED // 2),
    )(arrived, ref_sum, prior_mean, prior_precision, jnp.asarray(trend))


def on_device(
    interferograms, pseudo_inverse, date_pairs, ref_pixel, band_width, prior_mean, prior_precision
):
    n = lax.axis_size("rows")
    images, local_rows, columns = interferograms.shape
    fits = (columns // n) * local_rows == LANES and columns == HALVES * LANES and n % HALVES == 0
    fits = fits and local_rows == 2 * RADIUS and images == 600
    chosen = in_kernel if fits else in_steps
    return chosen(
        interferograms, pseudo_inverse, date_pairs, ref_pixel, band_width, prior_mean, prior_precision
    )


def solution(mesh):
    placed = (
        P(None, ("frame", "rows"), None),
        P(),
        P(),
        P("frame"),
        P(),
        P(("frame", "rows"), None, None),
        P(("frame", "rows"), None, None),
    )
    return jax.shard_map(
        on_device,
        mesh=mesh,
        in_specs=placed,
        out_specs=(
            P(("frame", "rows"), None, None),
            P(("frame", "rows"), None, None),
            P(("frame", "rows"), None),
        ),
        check_vma=False,
    )
```

```python
import functools
import math

import jax
import jax.numpy as jnp
import ml_dtypes
import numpy as np
from jax import lax
from jax.experimental import pallas as pl
from jax.experimental.pallas import tpu as pltpu
from jax.sharding import PartitionSpec as P

DATES = 200
RADIUS = 4
MESH = pl.DeviceIdType.MESH


def padded_2(cells, sides, width):
    for axis, dim in sides:
        count = lax.axis_size(axis)
        ends = count - 1
        head = lax.slice_in_dim(cells, 0, width, axis=dim)
        tail = lax.slice_in_dim(cells, cells.shape[dim] - width, cells.shape[dim], axis=dim)
        cells = jnp.concatenate(
            [
                lax.ppermute(tail, axis, [(i, (i + 1) % count) for i in range(ends)]),
                cells,
                lax.ppermute(head, axis, [((i + 1) % count, i) for i in range(ends)]),
            ],
            axis=dim,
        )
    return cells


def filter_taps(band_width):
    spread = band_width[0].astype(jnp.float32) / 10.0
    offsets = jnp.arange(-RADIUS, RADIUS + 1).astype(jnp.float32)
    raw_taps = jnp.exp(-offsets * offsets / (2.0 * spread * spread))
    return raw_taps / jnp.sum(raw_taps)


def column_pass(images, kernel_taps):
    values = images.astype(jnp.float32)
    columns = values.shape[2]
    padded = jnp.pad(values, ((0, 0), (0, 0), (RADIUS, RADIUS)))
    summed = kernel_taps[0] * padded[:, :, 0:columns]
    for offset in range(1, 2 * RADIUS + 1):
        summed = summed + kernel_taps[offset] * padded[:, :, offset : offset + columns]
    return summed.astype(jnp.bfloat16)


def row_pass(extended, kernel_taps, height):
    summed = kernel_taps[0] * extended[:, 0:height]
    for offset in range(1, 2 * RADIUS + 1):
        summed = summed + kernel_taps[offset] * extended[:, offset : offset + height]
    return summed


def design_of(date_pairs):
    date_index = jnp.arange(DATES, dtype=jnp.int32)
    later_date = (date_index[None, :] == date_pairs[1][:, None]).astype(jnp.float32)
    earlier = (date_index[None, :] == date_pairs[0][:, None]).astype(jnp.float32)
    return (later_date - earlier).astype(jnp.bfloat16)


def trend_basis():
    epochs = jnp.arange(DATES).astype(jnp.float32)
    centred = (epochs - (DATES - 1) / 2.0) / DATES
    annual_phase = 2.0 * math.pi * 12.0 / 365.25 * epochs
    constant = jnp.ones_like(epochs)
    return jnp.stack([constant, centred, jnp.cos(annual_phase), jnp.sin(annual_phase)], axis=1)


def misfit_of(slab_values, displacement, design):
    modelled = jnp.dot(design, displacement, preferred_element_type=jnp.float32)
    residual = slab_values.astype(jnp.float32) - modelled
    return jnp.mean(residual * residual, axis=0).astype(jnp.bfloat16)


def slab_major(values, slab_count, slab_cols):
    leading, local_rows, columns = values.shape
    split_up = values.reshape(leading, local_rows, slab_count, slab_cols).transpose(2, 0, 1, 3)
    return split_up.reshape(slab_count, leading, local_rows * slab_cols)


def from_sources(arrived):
    sources, leading, piece_len = arrived.shape
    return arrived.transpose(1, 0, 2).reshape(leading, sources * piece_len)


def solve_small(matrix, right_side):
    dimension = len(right_side)
    factor = [[None] * dimension for row_at in range(dimension)]
    for column_at in range(dimension):
        pivot_sq = matrix[column_at][column_at]
        for term_at in range(column_at):
            pivot_sq = pivot_sq - factor[column_at][term_at] * factor[column_at][term_at]
        factor[column_at][column_at] = jnp.sqrt(pivot_sq)
        for row_at in range(column_at + 1, dimension):
            element = matrix[row_at][column_at]
            for term_at in range(column_at):
                element = element - factor[row_at][term_at] * factor[column_at][term_at]
            factor[row_at][column_at] = element / factor[column_at][column_at]
    forward = []
    for row_at in range(dimension):
        element = right_side[row_at]
        for term_at in range(row_at):
            element = element - factor[row_at][term_at] * forward[term_at]
        forward.append(element / factor[row_at][row_at])
    solution = [None] * dimension
    for row_at in reversed(range(dimension)):
        element = forward[row_at]
        for term_at in range(row_at + 1, dimension):
            element = element - factor[term_at][row_at] * solution[term_at]
        solution[row_at] = element / factor[row_at][row_at]
    return solution


def kalman_update(series, misfit, prior_mean, prior_precision):
    trend_rows = trend_basis()
    trend_gram = jnp.dot(trend_rows.T, trend_rows, precision=lax.Precision.HIGHEST)
    projected = jnp.dot(trend_rows.T, series.astype(jnp.float32), precision=lax.Precision.HIGHEST)
    inverse_noise = 1.0 / (0.1 + misfit.astype(jnp.float32))
    matrix = [
        [
            trend_gram[row_at, column_at] * inverse_noise
            + (prior_precision[row_at] if row_at == column_at else 0.0)
            for column_at in range(4)
        ]
        for row_at in range(4)
    ]
    right_side = [
        prior_precision[row_at] * prior_mean[row_at] + projected[row_at] * inverse_noise
        for row_at in range(4)
    ]
    return jnp.stack(solve_small(matrix, right_side), axis=0)


def in_steps(
    interferograms, pseudo_inverse, date_pairs, ref_pixel, band_width, prior_mean, prior_precision
):
    kernel_taps = filter_taps(band_width)
    slab_count = lax.axis_size("rows")
    image_count, local_rows, columns = interferograms.shape
    slab_cols = columns // slab_count
    smoothed = lax.optimization_barrier(column_pass(interferograms, kernel_taps))
    extended = padded_2(smoothed, (("rows", 1),), RADIUS)
    lowpass = row_pass(extended.astype(jnp.float32), kernel_taps, local_rows)
    filtered = (interferograms.astype(jnp.float32) - lowpass).astype(jnp.bfloat16)
    design = design_of(date_pairs)
    values = filtered.reshape(image_count, local_rows * columns)
    displacement = jnp.dot(pseudo_inverse, values, preferred_element_type=jnp.float32).astype(
        jnp.bfloat16
    )
    misfit = misfit_of(values, displacement, design)
    ref_index = ref_pixel[0]
    ref_row = ref_index // columns
    ref_col = ref_index % columns
    owner = ref_row // local_rows
    local_pixel = (ref_row - owner * local_rows) * columns + ref_col
    own_series = lax.dynamic_slice_in_dim(displacement, local_pixel, 1, 1)[:, 0]
    own_term = jnp.where(lax.axis_index("rows") == owner, own_series.astype(jnp.float32), 0.0)
    ref_series = lax.psum(own_term, "rows")
    packed = jnp.concatenate([displacement, misfit[None]], axis=0)
    packed = packed.reshape(DATES + 1, local_rows, columns)
    arrived = from_sources(
        lax.all_to_all(
            slab_major(packed, slab_count, slab_cols), "rows", split_axis=0, concat_axis=0, tiled=True
        )
    )
    slab_disp, slab_misfit = arrived[:DATES], arrived[DATES]
    series = (slab_disp.astype(jnp.float32) - ref_series[:, None]).astype(jnp.bfloat16)
    kalman_state = kalman_update(series, slab_misfit, prior_mean[0], prior_precision[0])
    return (series[None], kalman_state[None], slab_misfit[None])


PAD_IMAGES = 608
PAD_DEPTH = 640
PAD_DATES = 208
LANES = 128
FINISH = 8
GROUP = 32
UNROLL = True
HALVES = 2
RAISED = 56 * 1024 * 1024


def split_three(values):
    first = values.astype(jnp.bfloat16)
    rest = values - first.astype(jnp.float32)
    second = rest.astype(jnp.bfloat16)
    third = (rest - second.astype(jnp.float32)).astype(jnp.bfloat16)
    return first, second, third


def dot_f32(left, right):
    return jnp.dot(left, right, preferred_element_type=jnp.float32)


def iota(shape, dim):
    return lax.broadcasted_iota(jnp.int32, shape, dim)


def column_of(lane, half, slab_cols):
    return (HALVES * (lane // slab_cols) + half) * slab_cols + lane % slab_cols


def kernel(
    n,
    ifg_ref,
    pinv_ref,
    pairs_ref,
    pixel_ref,
    band_ref,
    recv,
    ref_sum,
    by_row,
    weights,
    own,
    smooth,
    halo,
    filt,
    pinv_s,
    design_s,
    disp_s,
    sent,
    ref_out,
    ref_in,
    round_sem,
    halo_send,
    halo_recv,
    part_send,
    part_recv,
    ref_send,
    ref_recv,
    self_sem,
):
    local_rows, columns = filt.shape[1] // LANES, ifg_ref.shape[1]
    images = ifg_ref.shape[0] // local_rows
    slab_cols = columns // n
    per_half = n // HALVES
    me = lax.axis_index("rows")

    barrier = pltpu.get_barrier_semaphore()

    partners = [lax.rem(me + away, n) for away in (1, n - 1, 4, n - 4)]

    def greet(semaphore):
        for partner in partners:
            pl.semaphore_signal(semaphore, inc=1, device_id={"rows": partner}, device_id_type=MESH)

    greet(barrier)

    spread = jnp.full((8, LANES), band_ref[0], jnp.int32).astype(jnp.float32) / 10.0
    denominator = 2.0 * spread * spread
    raw = [jnp.exp(jnp.full((8, LANES), -float(k * k), jnp.float32) / denominator) for k in range(RADIUS + 1)]
    total = raw[0]
    for k in range(1, RADIUS + 1):
        total = total + 2.0 * raw[k]
    taps = [value / total for value in raw]
    lane = iota((columns, columns), 1)
    source = column_of(lane % LANES, lane // LANES, slab_cols)
    away = jnp.abs(iota((columns, columns), 0) - source)
    banded = jnp.zeros((columns, columns), jnp.float32)
    for k in range(RADIUS + 1):
        banded = jnp.where(away == k, taps[k][0:1, 0:1], banded)
    for at, piece in enumerate(split_three(banded)):
        weights[at] = piece
    weights[3] = jnp.where(away == 0, 1.0, 0.0).astype(jnp.bfloat16)

    size = GROUP * local_rows
    out_at, in_at = iota((size, size), 0), iota((size, size), 1)
    order = jnp.where((out_at % GROUP) * local_rows + out_at // GROUP == in_at, 1.0, 0.0).astype(jnp.bfloat16)

    def regroup(values, first):
        moved = dot_f32(order, values).astype(jnp.bfloat16)
        for r in range(local_rows):
            by_row[r, pl.ds(first, GROUP), :] = moved[r * GROUP : (r + 1) * GROUP]

    whole = images // GROUP

    @pl.loop(0, whole, unroll=UNROLL)
    def _(g):
        regroup(ifg_ref[pl.ds(pl.multiple_of(g * size, size), size), :], pl.multiple_of(g * GROUP, GROUP))

    left_over = images * local_rows - whole * size
    if left_over:
        values = ifg_ref[whole * size :, :]
        regroup(
            jnp.concatenate([values, jnp.zeros((size - left_over, columns), jnp.bfloat16)], axis=0),
            whole * GROUP,
        )

    def smooth_row(r):
        values = by_row[r]
        made = dot_f32(values, weights[0]) + dot_f32(values, weights[1]) + dot_f32(values, weights[2])
        made = made.astype(jnp.bfloat16)
        for h in range(HALVES):
            smooth[h, r] = made[:, h * LANES : (h + 1) * LANES]

    def halo_copy(down, h):
        rows = pl.ds(local_rows - RADIUS, RADIUS) if down else pl.ds(0, RADIUS)
        side = 0 if down else 1
        to = jnp.minimum(me + 1, n - 1) if down else jnp.maximum(me - 1, 0)
        return pltpu.make_async_remote_copy(
            src_ref=smooth.at[h, rows],
            dst_ref=halo.at[side, h],
            send_sem=halo_send.at[side, h],
            recv_sem=halo_recv.at[side, h],
            device_id={"rows": to},
            device_id_type=MESH,
        )

    pl.loop(local_rows - RADIUS, local_rows)(smooth_row)
    pl.semaphore_wait(barrier, len(partners))

    @pl.when(me < n - 1)
    def _():
        halo_copy(True, 0).start()

    pl.loop(0, local_rows - RADIUS)(smooth_row)

    @pl.when(me > 0)
    def _():
        halo_copy(False, 0).start()

    @pl.when(me < n - 1)
    def _():
        halo_copy(True, 1).start()

    @pl.when(me > 0)
    def _():
        halo_copy(False, 1).start()

    greet(round_sem.at[0])

    @pl.loop(0, local_rows)
    def _(r):
        made = dot_f32(by_row[r], weights[3]).astype(jnp.bfloat16)
        for h in range(HALVES):
            own[h, r] = made[:, h * LANES : (h + 1) * LANES]

    @pl.when(me == 0)
    def _():
        halo[0] = jnp.zeros(halo.shape[1:], halo.dtype)

    @pl.when(me == n - 1)
    def _():
        halo[1] = jnp.zeros(halo.shape[1:], halo.dtype)

    pl.semaphore_wait(round_sem.at[0], len(partners))
    greet(round_sem.at[1])

    pinv_s[...] = jnp.zeros_like(pinv_s)
    pinv_s[0:DATES, 0:images] = pinv_ref[...]
    date = iota((256, images), 0)
    later = jnp.where(date == pairs_ref[1:2, :], 1.0, 0.0)
    earlier = jnp.where(date == pairs_ref[0:1, :], 1.0, 0.0)
    both = jnp.concatenate([later - earlier, jnp.zeros((256, PAD_DEPTH - images), jnp.float32)], axis=1)
    design_s[...] = both.T.astype(jnp.bfloat16)
    filt[PAD_IMAGES:, :] = jnp.zeros((PAD_DEPTH - PAD_IMAGES, local_rows * LANES), jnp.bfloat16)

    pl.semaphore_wait(round_sem.at[1], len(partners))
    pixel = pixel_ref[0]
    ref_row, ref_col = pixel // columns, pixel % columns
    ref_total = jnp.zeros((16, 256), jnp.float32)
    block_lanes = 256

    def part_copy(h, k):
        q = lax.rem(me // HALVES + k, per_half)
        return pltpu.make_async_remote_copy(
            src_ref=sent.at[h, q],
            dst_ref=recv.at[me],
            send_sem=part_send.at[h, k],
            recv_sem=part_recv.at[me],
            device_id={"rows": HALVES * q + h},
            device_id_type=MESH,
        )

    def ref_copy(k):
        return pltpu.make_async_remote_copy(
            src_ref=ref_out,
            dst_ref=ref_in.at[me],
            send_sem=ref_send.at[k],
            recv_sem=ref_recv.at[me],
            device_id={"rows": lax.rem(me + k, n)},
            device_id_type=MESH,
        )

    for h in range(HALVES):

        @pl.when(me > 0)
        def _():
            halo_copy(True, h).wait_recv()

        @pl.when(me < n - 1)
        def _():
            halo_copy(False, h).wait_recv()

        @pl.loop(0, PAD_IMAGES // 16)
        def _(g):
            block = pl.ds(pl.multiple_of(g * 16, 16), 16)
            lines = [halo[0, h, t, block, :] for t in range(RADIUS)]
            lines += [smooth[h, r, block, :] for r in range(local_rows)]
            lines += [halo[1, h, t, block, :] for t in range(RADIUS)]
            lines = [line.astype(jnp.float32) for line in lines]
            for r in range(local_rows):
                low = lines[r + RADIUS] * taps[0][0:1]
                for k in range(1, RADIUS + 1):
                    low = low + (lines[r + RADIUS - k] + lines[r + RADIUS + k]) * taps[k][0:1]
                high = own[h, r, block, :].astype(jnp.float32) - low
                filt[block, r * LANES : (r + 1) * LANES] = high.astype(jnp.bfloat16)

        for b in range(local_rows * LANES // block_lanes):
            lanes = slice(b * block_lanes, (b + 1) * block_lanes)
            values = filt[:, lanes]
            disp = dot_f32(pinv_s[...], values).astype(jnp.bfloat16)
            disp_wide = jnp.concatenate([disp, jnp.zeros((256 - PAD_DATES, block_lanes), jnp.bfloat16)], axis=0)
            residual = values.astype(jnp.float32) - dot_f32(design_s[...], disp_wide)
            misfit = jnp.sum(residual * residual, axis=0, keepdims=True) / images
            at = iota((16, block_lanes), 1) + b * block_lanes
            hit = (at // LANES + me * local_rows == ref_row) & (column_of(at % LANES, h, slab_cols) == ref_col)
            ref_total += lax.dot_general(
                jnp.where(hit, 1.0, 0.0).astype(jnp.bfloat16),
                disp_wide,
                (((1,), (1,)), ((), ())),
                preferred_element_type=jnp.float32,
            )
            disp_s[0:DATES, lanes] = disp[0:DATES].astype(jnp.float32)
            disp_s[DATES:, lanes] = jnp.broadcast_to(misfit, (PAD_DATES - DATES, block_lanes))

        if h == HALVES - 1:
            ref_out[...] = ref_total.astype(jnp.bfloat16)

            @pl.loop(1, n)
            def _(k):
                ref_copy(k).start()

        @pl.loop(0, PAD_DATES // 16)
        def _(g):
            block = pl.ds(pl.multiple_of(g * 16, 16), 16)
            lines = [disp_s[block, r * LANES : (r + 1) * LANES] for r in range(local_rows)]
            place = iota((16, LANES), 1) // slab_cols
            for q in range(per_half):
                made = None
                for r in range(local_rows):
                    shift = ((r - q) * slab_cols) % LANES
                    moved = pltpu.roll(lines[r], shift, 1) if shift else lines[r]
                    made = moved if made is None else jnp.where(place == r, moved, made)
                sent[h, q, block, :] = made.astype(jnp.bfloat16)

        @pl.when(me % HALVES == h)
        def _():
            local = pltpu.make_async_copy(sent.at[h, me // HALVES], recv.at[me], self_sem)
            local.start()
            local.wait()

        @pl.when(me % HALVES != h)
        def _():
            part_copy(h, 0).start()

        @pl.loop(1, per_half)
        def _(k):
            part_copy(h, k).start()

    @pl.loop(1, n)
    def _(k):
        j = lax.rem(me + k, n)
        pltpu.make_async_remote_copy(
            src_ref=ref_out,
            dst_ref=ref_in.at[j],
            send_sem=ref_send.at[k],
            recv_sem=ref_recv.at[j],
            device_id={"rows": j},
            device_id_type=MESH,
        ).wait_recv()

    ref_in[me] = ref_out[...]
    total = ref_in[0].astype(jnp.float32)
    for j in range(1, n):
        total = total + ref_in[j].astype(jnp.float32)
    ref_sum[...] = total

    @pl.loop(1, n)
    def _(k):
        j = lax.rem(me + k, n)
        pltpu.make_async_remote_copy(
            src_ref=sent.at[0, 0],
            dst_ref=recv.at[j],
            send_sem=part_send.at[0, 0],
            recv_sem=part_recv.at[j],
            device_id={"rows": j},
            device_id_type=MESH,
        ).wait_recv()

    for h in range(HALVES):

        @pl.when(me < n - 1)
        def _():
            halo_copy(True, h).wait_send()

        @pl.when(me > 0)
        def _():
            halo_copy(False, h).wait_send()

        @pl.when(me % HALVES != h)
        def _():
            part_copy(h, 0).wait_send()

        @pl.loop(1, per_half)
        def _(k):
            part_copy(h, k).wait_send()

    @pl.loop(1, n)
    def _(k):
        ref_copy(k).wait_send()


def finish(gram, arrived, ref_sum, mean_ref, precision_ref, trend_ref, series_ref, state_ref, misfit_ref, proj):
    ref_column = jnp.broadcast_to(ref_sum[0:1], (LANES, 256)).T[0:PAD_DATES]
    for j in range(arrived.shape[0]):
        values = arrived[j].astype(jnp.float32)
        lanes = slice(j * LANES, (j + 1) * LANES)
        series = (values - ref_column).astype(jnp.bfloat16)
        series_ref[0, :, lanes] = series[0:DATES]
        made = dot_f32(trend_ref[...], series)
        proj[0:4, lanes] = made[0:4] + (made[4:8] + made[8:12])
        proj[4:5, lanes] = values[DATES : DATES + 1]

    misfit = proj[4:5, :]
    misfit_ref[...] = misfit.astype(jnp.bfloat16)
    inverse_noise = 1.0 / (0.1 + misfit)
    precision = [precision_ref[0, d : d + 1, :] for d in range(4)]
    matrix = [
        [float(gram[a][b]) * inverse_noise + (precision[a] if a == b else 0.0) for b in range(4)]
        for a in range(4)
    ]
    right_side = [precision[d] * mean_ref[0, d : d + 1, :] + proj[d : d + 1, :] * inverse_noise for d in range(4)]
    for d, value in enumerate(solve_small(matrix, right_side)):
        state_ref[0, d : d + 1, :] = value


def trend_constants():
    epochs = np.arange(DATES, dtype=np.float64)
    phase = 2.0 * np.pi * 12.0 / 365.25 * epochs
    rows = np.stack([np.ones_like(epochs), (epochs - (DATES - 1) / 2.0) / DATES, np.cos(phase), np.sin(phase)])
    return rows.astype(np.float32)


def in_kernel(interferograms, pseudo_inverse, date_pairs, ref_pixel, band_width, prior_mean, prior_precision):
    n = lax.axis_size("rows")
    images, local_rows, columns = interferograms.shape
    rows = trend_constants()
    gram = (rows.astype(np.float64) @ rows.astype(np.float64).T).astype(np.float32)
    pieces, rest = [], rows
    for _ in range(3):
        piece = rest.astype(ml_dtypes.bfloat16)
        pieces.append(piece)
        rest = rest - piece.astype(np.float32)
    trend = np.zeros((16, PAD_DATES), ml_dtypes.bfloat16)
    trend[0:12, 0:DATES] = np.concatenate(pieces, axis=0)
    vmem, smem = pl.BlockSpec(memory_space=pltpu.VMEM), pl.BlockSpec(memory_space=pltpu.SMEM)
    half_rows = (HALVES, local_rows, PAD_IMAGES, LANES)
    bf16, f32 = jnp.bfloat16, jnp.float32
    per_half = n // HALVES
    dma = pltpu.SemaphoreType.DMA
    arrived, ref_sum = pl.pallas_call(
        functools.partial(kernel, n),
        out_shape=(
            jax.ShapeDtypeStruct((n, PAD_DATES, LANES), bf16),
            jax.ShapeDtypeStruct((16, 256), f32),
        ),
        in_specs=[vmem, vmem, vmem, smem, smem],
        out_specs=(pl.BlockSpec(memory_space=pl.ANY), vmem),
        scratch_shapes=[
            pltpu.VMEM((local_rows, PAD_IMAGES, columns), bf16),
            pltpu.VMEM((4, columns, columns), bf16),
            pltpu.VMEM(half_rows, bf16),
            pltpu.VMEM(half_rows, bf16),
            pltpu.VMEM((2, HALVES, RADIUS, PAD_IMAGES, LANES), bf16),
            pltpu.VMEM((PAD_DEPTH, local_rows * LANES), bf16),
            pltpu.VMEM((PAD_DATES, PAD_DEPTH), bf16),
            pltpu.VMEM((PAD_DEPTH, 256), bf16),
            pltpu.VMEM((PAD_DATES, local_rows * LANES), f32),
            pltpu.VMEM((HALVES, per_half, PAD_DATES, LANES), bf16),
            pltpu.VMEM((16, 256), bf16),
            pltpu.VMEM((n, 16, 256), bf16),
            pltpu.SemaphoreType.REGULAR((2,)),
            dma((2, HALVES)),
            dma((2, HALVES)),
            dma((HALVES, per_half)),
            dma((n,)),
            dma((n,)),
            dma((n,)),
            dma,
        ],
        compiler_params=pltpu.CompilerParams(
            collective_id=0, has_side_effects=True, vmem_limit_bytes=RAISED
        ),
    )(
        interferograms.reshape(images * local_rows, columns),
        pseudo_inverse,
        date_pairs,
        ref_pixel,
        band_width,
    )
    return pl.pallas_call(
        functools.partial(finish, gram.tolist()),
        out_shape=(
            jax.ShapeDtypeStruct((1, DATES, n * LANES), bf16),
            jax.ShapeDtypeStruct((1, 4, n * LANES), f32),
            jax.ShapeDtypeStruct((1, n * LANES), bf16),
        ),
        grid=(n // FINISH,),
        in_specs=[
            pl.BlockSpec((FINISH, PAD_DATES, LANES), lambda g: (g, 0, 0)),
            vmem,
            pl.BlockSpec((1, 4, FINISH * LANES), lambda g: (0, 0, g)),
            pl.BlockSpec((1, 4, FINISH * LANES), lambda g: (0, 0, g)),
            vmem,
        ],
        out_specs=(
            pl.BlockSpec((1, DATES, FINISH * LANES), lambda g: (0, 0, g)),
            pl.BlockSpec((1, 4, FINISH * LANES), lambda g: (0, 0, g)),
            pl.BlockSpec((1, FINISH * LANES), lambda g: (0, g)),
        ),
        scratch_shapes=[pltpu.VMEM((8, FINISH * LANES), f32)],
        compiler_params=pltpu.CompilerParams(vmem_limit_bytes=RAISED // 2),
    )(arrived, ref_sum, prior_mean, prior_precision, jnp.asarray(trend))


def on_device(
    interferograms, pseudo_inverse, date_pairs, ref_pixel, band_width, prior_mean, prior_precision
):
    n = lax.axis_size("rows")
    images, local_rows, columns = interferograms.shape
    fits = (columns // n) * local_rows == LANES and columns == HALVES * LANES and n % HALVES == 0
    fits = fits and local_rows == 2 * RADIUS and images == 600
    chosen = in_kernel if fits else in_steps
    return chosen(
        interferograms, pseudo_inverse, date_pairs, ref_pixel, band_width, prior_mean, prior_precision
    )


def solution(mesh):
    placed = (
        P(None, ("frame", "rows"), None),
        P(),
        P(),
        P("frame"),
        P(),
        P(("frame", "rows"), None, None),
        P(("frame", "rows"), None, None),
    )
    return jax.shard_map(
        on_device,
        mesh=mesh,
        in_specs=placed,
        out_specs=(
            P(("frame", "rows"), None, None),
            P(("frame", "rows"), None, None),
            P(("frame", "rows"), None),
        ),
        check_vma=False,
    )
```
